256 devices in a mesh: blk: 256 (over x, y, z, core).
Axes of the slice: x: 4, y: 4, z: 8, core: 2. Of those that a mesh axis runs over, the one named last changes fastest.
Arguments:
- points: float32 [32768, 16], P('blk'), may hold values from -6 to 6, as said below
- lengthscale: float32 [16], replicated, may hold values from 1.2 to 2.5
- noise: float32 [32768], P('blk'), may hold values from 0.1 to 1
- solution: float32 [32768, 64], P('blk'), may hold values from -6 to 6
- residual: float32 [32768, 64], P('blk'), as said below
- direction: float32 [32768, 64], P('blk'), as said below
Outputs:
- new_solution: float32 [32768, 64], P('blk')
- new_residual: float32 [32768, 64], P('blk')
- new_direction: float32 [32768, 64], P('blk')
The draws below stay inside these ranges and needn't reach their ends.
Inputs may be any that keep to these rules, and one draw needn't show every extreme that they name: `points`: real-valued, of order one. `residual`: real-valued, of order one. `direction`: real-valued, of order one.
All inputs are finite; a program needn't handle non-finite values.
Results may differ from the reference program's by a relative error of at most 0.004.
Values may be sent and summed in bfloat16 or wider, within the bound.
A program may use at most 64 MiB of HBM per device.

```python
import math
import jax
import jax.numpy as jnp
from jax import lax

ROWS_DEV = 128
FEATURES = 16
PROBES = 64
POINTS = 32768
N_BLK = 256


def rough_field(key):
    rows = jnp.arange(POINTS).astype(jnp.float32)
    rise = jnp.exp(jnp.log(3.0) * rows / POINTS)[:, None]
    return jax.random.normal(key, (POINTS, PROBES), jnp.float32) * rise


def draw_points(key, part):
    key = jax.random.fold_in(key, 31)
    return jnp.clip(jax.random.normal(key, (POINTS, FEATURES), jnp.float32), -6.0, 6.0)


def draw_residual(key, part):
    key = jax.random.fold_in(key, 11)
    return rough_field(key)


def draw_direction(key, part):
    key = jax.random.fold_in(key, 23)
    return rough_field(key)


def block_levels(own_key, dims, pieces, low, largest):
    def one(axis_at, parts):
        heights = jax.random.uniform(jax.random.fold_in(jax.random.fold_in(own_key, 6), axis_at), (parts,), jnp.float32, low / len(pieces), largest / len(pieces))
        return jnp.repeat(jnp.exp(heights), dims[axis_at] // parts).reshape((-1,) + (1,) * (len(dims) - axis_at - 1))

    loudness = one(*pieces[0])
    for cut in pieces[1:]:
        loudness = loudness * one(*cut)
    return loudness


def scatter_about(key, extent, width, most, split=(), dtype=jnp.bfloat16):
    entries = jax.random.normal(key, extent, jnp.float32) * width
    if len(split) > 0:
        entries = block_levels(key, extent, split, -0.22, 0.18) * entries
    return jnp.clip(entries, min=-most, max=most).astype(dtype)


def setup_inputs(seed: int = 0) -> dict:
    splits = jax.random.split(jax.random.key(seed), 7)
    return {
        "points": draw_points(jax.random.fold_in(splits[6], 71), 0),
        "lengthscale": jnp.clip(jnp.exp(jax.random.uniform(splits[1], (FEATURES,), jnp.float32, math.log(1.2), math.log(2.5))), 1.2, 2.5),
        "noise": jnp.clip(jnp.exp(math.log(1.0) - 2.3025851 * jax.random.uniform(splits[2], (POINTS,), jnp.float32) ** block_levels(splits[2], (POINTS,), ((0, 256),), -0.2, 0.2)), 0.1, 1.0),
        "solution": scatter_about(splits[3], (POINTS, PROBES), 1.0, 6.0, ((0, 256),), jnp.float32),
        "residual": draw_residual(jax.random.fold_in(splits[6], 71), 0),
        "direction": draw_direction(jax.random.fold_in(splits[6], 71), 0),
    }


def kernel_tile(left, right):
    cross = lax.dot_general(left, right, (((1,), (1,)), ((), ())), precision=lax.Precision.HIGHEST, preferred_element_type=jnp.float32)
    dist = jnp.sum(left * left, axis=1)[:, None] + jnp.sum(right * right, axis=1)[None, :] - 2.0 * cross
    return jnp.exp(-0.5 * dist).astype(jnp.bfloat16)


def reference(points, lengthscale, noise, solution, residual, direction):
    scaled = points / lengthscale[None, :]
    dirb = direction.astype(jnp.bfloat16)
    block = ROWS_DEV * min(N_BLK, max(1, 512 // ROWS_DEV))
    starts = (jnp.arange(POINTS // block) * block).astype(jnp.int32)

    def rows(start):
        left = lax.dynamic_slice_in_dim(scaled, start, block, 0)
        return jnp.dot(kernel_tile(left, scaled), dirb, preferred_element_type=jnp.float32)

    product = lax.map(rows, starts).reshape(POINTS, PROBES)
    image = product + noise[:, None] * direction
    norm_old = jnp.sum(residual * residual, axis=0)
    curv = jnp.sum(direction * image, axis=0)
    alpha = norm_old / curv
    new_solution = solution + alpha[None, :] * direction
    new_residual = residual - alpha[None, :] * image
    norm_new = jnp.sum(new_residual * new_residual, axis=0)
    new_direction = new_residual + (norm_new / norm_old)[None, :] * direction
    return new_solution, new_residual, new_direction
```

```python
import functools
import math

import jax
import jax.numpy as jnp
from jax import lax
from jax.experimental import pallas as pl
from jax.experimental.pallas import tpu as pltpu
from jax.sharding import PartitionSpec as P

ROWS = 128
FEATURES = 16
PROBES = 64
X, Y, Z = 4, 4, 8
PLANE = X * Y
MSG = 2 * FEATURES + PROBES
FEAT = 5 * FEATURES
GROUP = 4
ROOT_LOG2E = math.sqrt(math.log2(math.e))
MESH = pl.DeviceIdType.MESH
BF = jnp.bfloat16
F32 = jnp.float32


def norm_rows(hi, lo, own_first):
    s = hi.astype(F32) + lo.astype(F32)
    n = -0.5 * jnp.sum(s * s, axis=0, keepdims=True)
    n1 = n.astype(BF).astype(F32)
    n2 = (n - n1).astype(BF).astype(F32)
    n3 = n - n1 - n2
    row = lax.broadcasted_iota(jnp.int32, (FEATURES, hi.shape[1]), 0)
    at = 0 if own_first else 3
    out = jnp.where((row >= 3 - at) & (row < 6 - at), 1.0, 0.0)
    for step, part in enumerate((n1, n2, n3)):
        out = jnp.where(row == at + step, part, out)
    return out.astype(BF)


def row_features(hi, lo):
    return jnp.concatenate([hi, hi, lo, lo, norm_rows(hi, lo, True)], axis=0)


def col_features(hi, lo):
    return jnp.concatenate([hi, lo, hi, lo, norm_rows(hi, lo, False)], axis=0)


def total_lanes(v):
    return jnp.sum(v, axis=1, keepdims=True)


def pack(lane, cols, first, out):
    for t in range(PROBES // 8):
        out = jnp.where(lane == first + t, cols[8 * t : 8 * t + 8], out)
    return out


def body(
    pts, ls, noise, sol, res, dirn,
    o_sol, o_res, o_dir,
    v_pts, v_ls, v_noise, v_sol, v_res, v_dir,
    rowbuf, colbuf, feat, acc, part, ar1, ar2,
    in_sem, row_s, row_r, col_s, col_r, sib_s, sib_r, rs_s, rs_r, a1_s, a1_r, a2_s, a2_r,
):
    me = lax.axis_index("blk")
    c = lax.rem(me, 2)
    z = lax.rem(me // 2, Z)
    y = lax.rem(me // (2 * Z), Y)
    x = me // (2 * Z * Y)

    def at(dx, dy, dz, dc):
        cc = c if dc == 0 else 1 - c
        zz = lax.rem(z + dz, Z)
        yy = lax.rem(y + dy, Y)
        xx = lax.rem(x + dx, X)
        return ((xx * Y + yy) * Z + zz) * 2 + cc

    plane = [(k // Y, k % Y) for k in range(PLANE)]
    column = [(k % Z, k // Z) for k in range(2 * Z)]
    plane_id = [at(dx, dy, 0, 0) for dx, dy in plane]
    column_id = [at(0, 0, dz, dc) for dz, dc in column]

    def remote(src, dst, s, r, dev):
        return pltpu.make_async_remote_copy(
            src_ref=src, dst_ref=dst, send_sem=s, recv_sem=r, device_id=(dev,), device_id_type=MESH
        )

    loads = [
        pltpu.make_async_copy(src, dst, in_sem.at[i])
        for i, (src, dst) in enumerate(
            ((pts, v_pts), (ls, v_ls), (dirn, v_dir), (res, v_res), (noise, v_noise), (sol, v_sol))
        )
    ]
    for load in loads:
        load.start()
    barrier = pltpu.get_barrier_semaphore()
    for dev in plane_id[1:] + column_id[1:]:
        pl.semaphore_signal(barrier, inc=1, device_id=(dev,), device_id_type=MESH)

    loads[0].wait()
    loads[1].wait()
    eye = lax.broadcasted_iota(jnp.int32, (FEATURES, FEATURES), 0) == lax.broadcasted_iota(
        jnp.int32, (FEATURES, FEATURES), 1
    )
    scale = total_lanes(jnp.where(eye, jnp.broadcast_to(v_ls[...], (FEATURES, FEATURES)), 0.0))
    scaled = v_pts[...] / scale * ROOT_LOG2E
    hi = scaled.astype(BF)
    lo = (scaled - hi.astype(F32)).astype(BF)
    rowbuf[0, 0:FEATURES] = hi
    rowbuf[0, FEATURES : 2 * FEATURES] = lo
    colbuf[0, 0, 0:FEATURES] = hi
    colbuf[0, 0, FEATURES : 2 * FEATURES] = lo
    loads[2].wait()
    colbuf[0, 0, 2 * FEATURES : MSG] = v_dir[...].astype(BF)

    pl.semaphore_wait(barrier, 30)
    rows = [
        remote(rowbuf.at[0], rowbuf.at[Z - k], row_s.at[k], row_r.at[Z - k], column_id[k])
        for k in range(1, Z)
    ]
    for copy in rows:
        copy.start()
    cols = []
    for k in range(1, PLANE):
        dx, dy = plane[k]
        slot = ((X - dx) % X) * Y + (Y - dy) % Y
        cols.append(
            remote(colbuf.at[0, 0], colbuf.at[0, slot], col_s.at[k], col_r.at[slot], plane_id[k])
        )
    for copy in cols:
        copy.start()

    for load in loads[3:]:
        load.wait()
    lane = lax.broadcasted_iota(jnp.int32, (8, 128), 1)
    sums = pack(lane, total_lanes(v_res[...] * v_res[...]), 0, jnp.zeros((8, 128), F32))

    feat[:, 0:ROWS] = row_features(rowbuf[0, 0:FEATURES], rowbuf[0, FEATURES : 2 * FEATURES])
    for k in range(1, Z):
        remote(rowbuf.at[0], rowbuf.at[k], row_s.at[k], row_r.at[k], column_id[k]).wait_recv()
    for k in range(1, Z):
        feat[:, k * ROWS : (k + 1) * ROWS] = row_features(
            rowbuf[k, 0:FEATURES], rowbuf[k, FEATURES : 2 * FEATURES]
        )

    def product(half, first, rows_at, rows_n):
        blocks = range(first, first + GROUP)
        b = jnp.concatenate(
            [
                col_features(colbuf[half, j, 0:FEATURES], colbuf[half, j, FEATURES : 2 * FEATURES])
                for j in blocks
            ],
            axis=1,
        )
        d = jnp.concatenate([colbuf[half, j, 2 * FEATURES : MSG] for j in blocks], axis=1)
        s = lax.dot_general(
            b, feat[:, rows_at : rows_at + rows_n], (((0,), (0,)), ((), ())), preferred_element_type=F32
        )
        return jnp.dot(d, jnp.exp2(s).astype(BF), preferred_element_type=F32)

    forwards = []
    for g in range(PLANE // GROUP):
        for slot in range(g * GROUP, (g + 1) * GROUP):
            if slot:
                remote(
                    colbuf.at[0, 0], colbuf.at[0, slot], col_s.at[slot], col_r.at[slot], plane_id[slot]
                ).wait_recv()
        part_of = pl.ds(g * GROUP, GROUP)
        forward = remote(
            colbuf.at[0, part_of], colbuf.at[1, part_of], sib_s.at[g], sib_r.at[g], column_id[Z]
        )
        forward.start()
        forwards.append(forward)
        q = product(0, g * GROUP, 0, Z * ROWS)
        if g == 0:
            acc[...] = q
        else:
            acc[...] += q
    for g in range(PLANE // GROUP):
        forwards[g].wait_recv()
        acc[...] += product(1, g * GROUP, 0, Z * ROWS)

    for k in range(1, Z):
        part[k] = acc[:, k * ROWS : (k + 1) * ROWS]
    homes = [
        remote(part.at[k], part.at[2 * Z - k], rs_s.at[k], rs_r.at[Z - k], column_id[k])
        for k in range(1, Z)
    ]
    for copy in homes:
        copy.start()
    image = acc[:, 0:ROWS] + v_noise[...] * v_dir[...]
    for k in range(1, Z):
        remote(part.at[k], part.at[Z + k], rs_s.at[k], rs_r.at[k], column_id[k]).wait_recv()
    for k in range(1, Z):
        image += part[Z + k]

    sums = pack(lane, total_lanes(v_dir[...] * image), 8, sums)
    sums = pack(lane, total_lanes(v_res[...] * image), 16, sums)
    sums = pack(lane, total_lanes(image * image), 24, sums)

    ar1[0] = sums
    firsts = []
    for k in range(1, 2 * Z):
        dz, dc = column[k]
        slot = (Z - dz) % Z + dc * Z
        firsts.append(remote(ar1.at[0], ar1.at[slot], a1_s.at[k], a1_r.at[slot], column_id[k]))
    for copy in firsts:
        copy.start()
    for k in range(1, 2 * Z):
        remote(ar1.at[0], ar1.at[k], a1_s.at[k], a1_r.at[k], column_id[k]).wait_recv()
    ar2[0] = jnp.sum(ar1[...], axis=0)
    seconds = []
    for k in range(1, PLANE):
        dx, dy = plane[k]
        slot = ((X - dx) % X) * Y + (Y - dy) % Y
        seconds.append(remote(ar2.at[0], ar2.at[slot], a2_s.at[k], a2_r.at[slot], plane_id[k]))
    for copy in seconds:
        copy.start()
    for k in range(1, PLANE):
        remote(ar2.at[0], ar2.at[k], a2_s.at[k], a2_r.at[k], plane_id[k]).wait_recv()
    total = jnp.sum(ar2[...], axis=0)

    alpha = total / pltpu.roll(total, 120, 1)
    change = alpha * (alpha * pltpu.roll(total, 104, 1) - 2.0 * pltpu.roll(total, 112, 1))
    beta = (total + change) / total
    for t in range(PROBES // 8):
        at8 = slice(8 * t, 8 * t + 8)
        a = alpha[:, t : t + 1]
        new = v_res[at8] - a * image[at8]
        o_res[at8] = new
        o_sol[at8] = v_sol[at8] + a * v_dir[at8]
        o_dir[at8] = new + beta[:, t : t + 1] * v_dir[at8]

    for copy in rows + cols + forwards + homes + firsts + seconds:
        copy.wait_send()


def per_device(points, lengthscale, noise, solution, residual, direction):
    sems = pltpu.SemaphoreType.DMA
    out = jax.ShapeDtypeStruct((PROBES, ROWS), F32)
    hbm = pl.BlockSpec(memory_space=pltpu.HBM)
    vmem = pl.BlockSpec(memory_space=pltpu.VMEM)
    outs = pl.pallas_call(
        body,
        out_shape=(out, out, out),
        in_specs=[hbm] * 6,
        out_specs=(vmem, vmem, vmem),
        scratch_shapes=[
            pltpu.VMEM((FEATURES, ROWS), F32),
            pltpu.VMEM((1, FEATURES), F32),
            pltpu.VMEM((1, ROWS), F32),
            pltpu.VMEM((PROBES, ROWS), F32),
            pltpu.VMEM((PROBES, ROWS), F32),
            pltpu.VMEM((PROBES, ROWS), F32),
            pltpu.VMEM((Z, 2 * FEATURES, ROWS), BF),
            pltpu.VMEM((2, PLANE, MSG, ROWS), BF),
            pltpu.VMEM((FEAT, Z * ROWS), BF),
            pltpu.VMEM((PROBES, Z * ROWS), F32),
            pltpu.VMEM((2 * Z, PROBES, ROWS), F32),
            pltpu.VMEM((2 * Z, 8, 128), F32),
            pltpu.VMEM((PLANE, 8, 128), F32),
            sems((6,)),
            sems((Z,)), sems((Z,)),
            sems((PLANE,)), sems((PLANE,)),
            sems((PLANE // GROUP,)), sems((PLANE // GROUP,)),
            sems((Z,)), sems((Z,)),
            sems((2 * Z,)), sems((2 * Z,)),
            sems((PLANE,)), sems((PLANE,)),
        ],
        compiler_params=pltpu.CompilerParams(
            collective_id=0, has_side_effects=True, vmem_limit_bytes=32 << 20
        ),
    )(
        points.T, lengthscale[None, :], noise[None, :], solution.T, residual.T, direction.T
    )
    return tuple(o.T for o in outs)


def solution(mesh):
    placed = (P("blk", None), P(), P("blk"), P("blk", None), P("blk", None), P("blk", None))
    return jax.shard_map(
        per_device,
        mesh=mesh,
        in_specs=placed,
        out_specs=(P("blk", None), P("blk", None), P("blk", None)),
        check_vma=False,
    )
```

```python
import functools
import math

import jax
import jax.numpy as jnp
from jax import lax
from jax.experimental import pallas as pl
from jax.experimental.pallas import tpu as pltpu
from jax.sharding import PartitionSpec as P

ROWS = 128
FEATURES = 16
PROBES = 64
X, Y, Z = 4, 4, 8
PLANE = X * Y
MSG = 2 * FEATURES + PROBES
FEAT = 5 * FEATURES
GROUP = 4
ROOT_LOG2E = math.sqrt(math.log2(math.e))
MESH = pl.DeviceIdType.MESH
BF = jnp.bfloat16
F32 = jnp.float32


def norm_rows(hi, lo, own_first):
    s = hi.astype(F32) + lo.astype(F32)
    n = -0.5 * jnp.sum(s * s, axis=0, keepdims=True)
    n1 = n.astype(BF).astype(F32)
    n2 = (n - n1).astype(BF).astype(F32)
    n3 = n - n1 - n2
    row = lax.broadcasted_iota(jnp.int32, (FEATURES, hi.shape[1]), 0)
    at = 0 if own_first else 3
    out = jnp.where((row >= 3 - at) & (row < 6 - at), 1.0, 0.0)
    for step, part in enumerate((n1, n2, n3)):
        out = jnp.where(row == at + step, part, out)
    return out.astype(BF)


def row_features(hi, lo):
    return jnp.concatenate([hi, hi, lo, lo, norm_rows(hi, lo, True)], axis=0)


def col_features(hi, lo):
    return jnp.concatenate([hi, lo, hi, lo, norm_rows(hi, lo, False)], axis=0)


def total_lanes(v):
    return jnp.sum(v, axis=1, keepdims=True)


def pack(lane, cols, first, out):
    for t in range(PROBES // 8):
        out = jnp.where(lane == first + t, cols[8 * t : 8 * t + 8], out)
    return out


def body(
    pts, ls, noise, res, dirn,
    o_image, o_alpha, o_beta,
    v_pts, v_ls, v_noise, v_res, v_dir,
    rowbuf, colbuf, feat, acc, part, ar1, ar2,
    in_sem, row_s, row_r, col_s, col_r, sib_s, sib_r, rs_s, rs_r, a1_s, a1_r, a2_s, a2_r,
):
    me = lax.axis_index("blk")
    c = lax.rem(me, 2)
    z = lax.rem(me // 2, Z)
    y = lax.rem(me // (2 * Z), Y)
    x = me // (2 * Z * Y)

    def at(dx, dy, dz, dc):
        cc = c if dc == 0 else 1 - c
        zz = lax.rem(z + dz, Z)
        yy = lax.rem(y + dy, Y)
        xx = lax.rem(x + dx, X)
        return ((xx * Y + yy) * Z + zz) * 2 + cc

    def hops(dx, dy, dz):
        return min(dx, X - dx) + min(dy, Y - dy) + min(dz, Z - dz)

    plane = sorted(((k // Y, k % Y) for k in range(PLANE)), key=lambda o: hops(o[0], o[1], 0))
    ring = sorted(range(Z), key=lambda dz: hops(0, 0, dz))
    column = sorted(((dz, dc) for dz in range(Z) for dc in range(2)), key=lambda o: 2 * hops(0, 0, o[0]) + o[1])
    plane_id = [at(dx, dy, 0, 0) for dx, dy in plane]
    ring_id = [at(0, 0, dz, 0) for dz in ring]
    column_id = [at(0, 0, dz, dc) for dz, dc in column]
    sibling = at(0, 0, 0, 1)
    plane_back = [plane.index(((X - dx) % X, (Y - dy) % Y)) for dx, dy in plane]
    ring_back = [ring.index((Z - dz) % Z) for dz in ring]
    column_back = [column.index(((Z - dz) % Z, dc)) for dz, dc in column]

    def remote(src, dst, s, r, dev):
        return pltpu.make_async_remote_copy(
            src_ref=src, dst_ref=dst, send_sem=s, recv_sem=r, device_id=(dev,), device_id_type=MESH
        )

    loads = [
        pltpu.make_async_copy(src, dst, in_sem.at[i])
        for i, (src, dst) in enumerate(
            ((pts, v_pts), (ls, v_ls), (dirn, v_dir), (res, v_res), (noise, v_noise))
        )
    ]
    for load in loads:
        load.start()
    barrier = pltpu.get_barrier_semaphore()
    for dev in ring_id[:0:-1] + plane_id[:0:-1] + [sibling]:
        pl.semaphore_signal(barrier, inc=1, device_id=(dev,), device_id_type=MESH)

    loads[0].wait()
    loads[1].wait()
    eye = lax.broadcasted_iota(jnp.int32, (FEATURES, FEATURES), 0) == lax.broadcasted_iota(
        jnp.int32, (FEATURES, FEATURES), 1
    )
    scale = total_lanes(jnp.where(eye, jnp.broadcast_to(v_ls[...], (FEATURES, FEATURES)), 0.0))
    scaled = v_pts[...] / scale * ROOT_LOG2E
    hi = scaled.astype(BF)
    lo = (scaled - hi.astype(F32)).astype(BF)
    rowbuf[0, 0:FEATURES] = hi
    rowbuf[0, FEATURES : 2 * FEATURES] = lo
    colbuf[0, 0, 0:FEATURES] = hi
    colbuf[0, 0, FEATURES : 2 * FEATURES] = lo
    loads[2].wait()
    colbuf[0, 0, 2 * FEATURES : MSG] = v_dir[...].astype(BF)

    pl.semaphore_wait(barrier, PLANE + Z - 1)
    rows = [
        remote(rowbuf.at[0], rowbuf.at[ring_back[k]], row_s.at[k], row_r.at[ring_back[k]], ring_id[k])
        for k in range(Z - 1, 0, -1)
    ]
    cols = [
        remote(
            colbuf.at[0, 0], colbuf.at[0, plane_back[k]], col_s.at[k], col_r.at[plane_back[k]], plane_id[k]
        )
        for k in range(PLANE - 1, 0, -1)
    ]
    for copy in rows + cols:
        copy.start()

    for load in loads[3:]:
        load.wait()
    lane = lax.broadcasted_iota(jnp.int32, (8, 128), 1)
    sums = pack(lane, total_lanes(v_res[...] * v_res[...]), 0, jnp.zeros((8, 128), F32))

    def rows_in(first, last):
        for k in range(max(first, 1), last):
            remote(rowbuf.at[0], rowbuf.at[k], row_s.at[k], row_r.at[k], ring_id[k]).wait_recv()
        for k in range(first, last):
            feat[:, k * ROWS : (k + 1) * ROWS] = row_features(
                rowbuf[k, 0:FEATURES], rowbuf[k, FEATURES : 2 * FEATURES]
            )

    def cols_in(g):
        for k in range(max(g * GROUP, 1), (g + 1) * GROUP):
            remote(colbuf.at[0, 0], colbuf.at[0, k], col_s.at[k], col_r.at[k], plane_id[k]).wait_recv()
        here = pl.ds(g * GROUP, GROUP)
        copy = remote(colbuf.at[0, here], colbuf.at[1, here], sib_s.at[g], sib_r.at[g], sibling)
        copy.start()
        return copy

    def product(half, first, rows_at, rows_n):
        blocks = range(first, first + GROUP)
        b = jnp.concatenate(
            [
                col_features(colbuf[half, j, 0:FEATURES], colbuf[half, j, FEATURES : 2 * FEATURES])
                for j in blocks
            ],
            axis=1,
        )
        d = jnp.concatenate([colbuf[half, j, 2 * FEATURES : MSG] for j in blocks], axis=1)
        s = lax.dot_general(
            b, feat[:, rows_at : rows_at + rows_n], (((0,), (0,)), ((), ())), preferred_element_type=F32
        )
        return jnp.dot(d, jnp.exp2(s).astype(BF), preferred_element_type=F32)

    half = Z * ROWS // 2
    forwards = [cols_in(0)]
    rows_in(0, Z // 2)
    acc[:, 0:half] = product(0, 0, 0, half)
    forwards.append(cols_in(1))
    acc[:, 0:half] += product(0, GROUP, 0, half)
    rows_in(Z // 2, Z)
    forwards.append(cols_in(2))
    acc[:, half:] = product(0, 0, half, half) + product(0, GROUP, half, half)
    forwards.append(cols_in(3))
    acc[...] += product(0, 2 * GROUP, 0, 2 * half)
    acc[...] += product(0, 3 * GROUP, 0, 2 * half)
    for g in range(PLANE // GROUP):
        forwards[g].wait_recv()
        acc[...] += product(1, g * GROUP, 0, 2 * half)

    homes = []
    for k in range(Z - 1, 0, -1):
        part[k] = acc[:, k * ROWS : (k + 1) * ROWS].astype(BF)
        copy = remote(part.at[k], part.at[Z + ring_back[k]], rs_s.at[k], rs_r.at[ring_back[k]], ring_id[k])
        copy.start()
        homes.append(copy)
    image = acc[:, 0:ROWS] + v_noise[...] * v_dir[...]
    for k in range(1, Z):
        remote(part.at[k], part.at[Z + k], rs_s.at[k], rs_r.at[k], ring_id[k]).wait_recv()
        image += part[Z + k].astype(F32)

    sums = pack(lane, total_lanes(v_dir[...] * image), 8, sums)
    sums = pack(lane, total_lanes(v_res[...] * image), 16, sums)
    sums = pack(lane, total_lanes(image * image), 24, sums)

    ar1[0] = sums
    firsts = [
        remote(ar1.at[0], ar1.at[column_back[k]], a1_s.at[k], a1_r.at[column_back[k]], column_id[k])
        for k in range(2 * Z - 1, 0, -1)
    ]
    for copy in firsts:
        copy.start()
    for k in range(1, 2 * Z):
        remote(ar1.at[0], ar1.at[k], a1_s.at[k], a1_r.at[k], column_id[k]).wait_recv()
    ar2[0] = jnp.sum(ar1[...], axis=0)
    seconds = [
        remote(ar2.at[0], ar2.at[plane_back[k]], a2_s.at[k], a2_r.at[plane_back[k]], plane_id[k])
        for k in range(PLANE - 1, 0, -1)
    ]
    for copy in seconds:
        copy.start()
    for k in range(1, PLANE):
        remote(ar2.at[0], ar2.at[k], a2_s.at[k], a2_r.at[k], plane_id[k]).wait_recv()
    total = jnp.sum(ar2[...], axis=0)

    alpha = total / pltpu.roll(total, 120, 1)
    change = alpha * (alpha * pltpu.roll(total, 104, 1) - 2.0 * pltpu.roll(total, 112, 1))
    beta = (total + change) / total
    for t in range(PROBES // 8):
        at8 = slice(8 * t, 8 * t + 8)
        o_alpha[at8] = jnp.broadcast_to(alpha[:, t : t + 1], (8, ROWS))
        o_beta[at8] = jnp.broadcast_to(beta[:, t : t + 1], (8, ROWS))
    o_image[...] = image

    for copy in rows + cols + forwards + homes + firsts + seconds:
        copy.wait_send()


def per_device(points, lengthscale, noise, solution, residual, direction):
    sems = pltpu.SemaphoreType.DMA
    out = jax.ShapeDtypeStruct((PROBES, ROWS), F32)
    hbm = pl.BlockSpec(memory_space=pltpu.HBM)
    vmem = pl.BlockSpec(memory_space=pltpu.VMEM)
    image, alpha, beta = pl.pallas_call(
        body,
        out_shape=(out, out, out),
        in_specs=[hbm] * 5,
        out_specs=(vmem, vmem, vmem),
        scratch_shapes=[
            pltpu.VMEM((FEATURES, ROWS), F32),
            pltpu.VMEM((1, FEATURES), F32),
            pltpu.VMEM((1, ROWS), F32),
            pltpu.VMEM((PROBES, ROWS), F32),
            pltpu.VMEM((PROBES, ROWS), F32),
            pltpu.VMEM((Z, 2 * FEATURES, ROWS), BF),
            pltpu.VMEM((2, PLANE, MSG, ROWS), BF),
            pltpu.VMEM((FEAT, Z * ROWS), BF),
            pltpu.VMEM((PROBES, Z * ROWS), F32),
            pltpu.VMEM((2 * Z, PROBES, ROWS), BF),
            pltpu.VMEM((2 * Z, 8, 128), F32),
            pltpu.VMEM((PLANE, 8, 128), F32),
            sems((5,)),
            sems((Z,)), sems((Z,)),
            sems((PLANE,)), sems((PLANE,)),
            sems((PLANE // GROUP,)), sems((PLANE // GROUP,)),
            sems((Z,)), sems((Z,)),
            sems((2 * Z,)), sems((2 * Z,)),
            sems((PLANE,)), sems((PLANE,)),
        ],
        compiler_params=pltpu.CompilerParams(
            collective_id=0, has_side_effects=True, vmem_limit_bytes=60 << 20
        ),
    )(
        points.T, lengthscale[None, :], noise[None, :], residual.T, direction.T
    )
    new_residual = residual - alpha.T * image.T
    return (
        solution + alpha.T * direction,
        new_residual,
        new_residual + beta.T * direction,
    )


def solution(mesh):
    placed = (P("blk", None), P(), P("blk"), P("blk", None), P("blk", None), P("blk", None))
    return jax.shard_map(
        per_device,
        mesh=mesh,
        in_specs=placed,
        out_specs=(P("blk", None), P("blk", None), P("blk", None)),
        check_vma=False,
    )
```

```python
import functools
import math

import jax
import jax.numpy as jnp
from jax import lax
from jax.experimental import pallas as pl
from jax.experimental.pallas import tpu as pltpu
from jax.sharding import PartitionSpec as P

ROWS = 128
FEATURES = 16
PROBES = 64
X, Y, Z = 4, 4, 8
PLANE = X * Y
MSG = 2 * FEATURES + PROBES
FEAT = 5 * FEATURES
GROUP = 4
ROOT_LOG2E = math.sqrt(math.log2(math.e))
MESH = pl.DeviceIdType.MESH
BF = jnp.bfloat16
F32 = jnp.float32


def norm_rows(hi, lo, own_first):
    s = hi.astype(F32) + lo.astype(F32)
    n = -0.5 * jnp.sum(s * s, axis=0, keepdims=True)
    n1 = n.astype(BF).astype(F32)
    n2 = (n - n1).astype(BF).astype(F32)
    n3 = n - n1 - n2
    row = lax.broadcasted_iota(jnp.int32, (FEATURES, hi.shape[1]), 0)
    at = 0 if own_first else 3
    out = jnp.where((row >= 3 - at) & (row < 6 - at), 1.0, 0.0)
    for step, part in enumerate((n1, n2, n3)):
        out = jnp.where(row == at + step, part, out)
    return out.astype(BF)


def row_features(hi, lo):
    return jnp.concatenate([hi, hi, lo, lo, norm_rows(hi, lo, True)], axis=0)


def col_features(hi, lo):
    return jnp.concatenate([hi, lo, hi, lo, norm_rows(hi, lo, False)], axis=0)


def total_lanes(v):
    return jnp.sum(v, axis=1, keepdims=True)


def pack(lane, cols, first, out):
    for t in range(PROBES // 8):
        out = jnp.where(lane == first + t, cols[8 * t : 8 * t + 8], out)
    return out


def body(
    pts, ls, noise, sol, res, dirn,
    v_sol, v_res, o_move, o_drop, o_push,
    v_pts, v_ls, v_noise, v_dir,
    rowbuf, colbuf, feat, acc, part, ar1, ar2,
    in_sem, row_s, row_r, col_s, col_r, sib_s, sib_r, rs_s, rs_r, a1_s, a1_r, a2_s, a2_r,
):
    me = lax.axis_index("blk")
    c = lax.rem(me, 2)
    z = lax.rem(me // 2, Z)
    y = lax.rem(me // (2 * Z), Y)
    x = me // (2 * Z * Y)

    def at(dx, dy, dz, dc):
        cc = c if dc == 0 else 1 - c
        zz = lax.rem(z + dz, Z)
        yy = lax.rem(y + dy, Y)
        xx = lax.rem(x + dx, X)
        return ((xx * Y + yy) * Z + zz) * 2 + cc

    def hops(dx, dy, dz):
        return min(dx, X - dx) + min(dy, Y - dy) + min(dz, Z - dz)

    plane = sorted(((k // Y, k % Y) for k in range(PLANE)), key=lambda o: hops(o[0], o[1], 0))
    ring = sorted(range(Z), key=lambda dz: hops(0, 0, dz))
    column = sorted(((dz, dc) for dz in range(Z) for dc in range(2)), key=lambda o: 2 * hops(0, 0, o[0]) + o[1])
    plane_id = [at(dx, dy, 0, 0) for dx, dy in plane]
    ring_id = [at(0, 0, dz, 0) for dz in ring]
    column_id = [at(0, 0, dz, dc) for dz, dc in column]
    sibling = at(0, 0, 0, 1)
    plane_back = [plane.index(((X - dx) % X, (Y - dy) % Y)) for dx, dy in plane]
    ring_back = [ring.index((Z - dz) % Z) for dz in ring]
    column_back = [column.index(((Z - dz) % Z, dc)) for dz, dc in column]

    def remote(src, dst, s, r, dev):
        return pltpu.make_async_remote_copy(
            src_ref=src, dst_ref=dst, send_sem=s, recv_sem=r, device_id=(dev,), device_id_type=MESH
        )

    barrier = pltpu.get_barrier_semaphore()
    for dev in ring_id[:0:-1] + plane_id[:0:-1] + [sibling]:
        pl.semaphore_signal(barrier, inc=1, device_id=(dev,), device_id_type=MESH)
    loads = [
        pltpu.make_async_copy(src, dst, in_sem.at[i])
        for i, (src, dst) in enumerate(
            ((pts, v_pts), (ls, v_ls), (dirn, v_dir), (res, v_res), (noise, v_noise), (sol, v_sol))
        )
    ]
    for load in loads:
        load.start()

    loads[0].wait()
    loads[1].wait()
    eye = lax.broadcasted_iota(jnp.int32, (FEATURES, FEATURES), 0) == lax.broadcasted_iota(
        jnp.int32, (FEATURES, FEATURES), 1
    )
    scale = total_lanes(jnp.where(eye, jnp.broadcast_to(v_ls[...], (FEATURES, FEATURES)), 0.0))
    scaled = v_pts[...] / scale * ROOT_LOG2E
    hi = scaled.astype(BF)
    lo = (scaled - hi.astype(F32)).astype(BF)
    rowbuf[0, 0:FEATURES] = hi
    rowbuf[0, FEATURES : 2 * FEATURES] = lo
    colbuf[0, 0, 0:FEATURES] = hi
    colbuf[0, 0, FEATURES : 2 * FEATURES] = lo
    loads[2].wait()
    colbuf[0, 0, 2 * FEATURES : MSG] = v_dir[...].astype(BF)

    pl.semaphore_wait(barrier, PLANE + Z - 1)
    rows = [
        remote(rowbuf.at[0], rowbuf.at[ring_back[k]], row_s.at[k], row_r.at[ring_back[k]], ring_id[k])
        for k in range(Z - 1, 0, -1)
    ]
    cols = [
        remote(
            colbuf.at[0, 0], colbuf.at[0, plane_back[k]], col_s.at[k], col_r.at[plane_back[k]], plane_id[k]
        )
        for k in range(1, PLANE)
    ]
    for copy in rows + cols:
        copy.start()

    for load in loads[3:]:
        load.wait()
    lane = lax.broadcasted_iota(jnp.int32, (8, 128), 1)
    sums = pack(lane, total_lanes(v_res[...] * v_res[...]), 0, jnp.zeros((8, 128), F32))

    def rows_in():
        for k in range(1, Z):
            remote(rowbuf.at[0], rowbuf.at[k], row_s.at[k], row_r.at[k], ring_id[k]).wait_recv()
        for k in range(Z):
            feat[:, k * ROWS : (k + 1) * ROWS] = row_features(
                rowbuf[k, 0:FEATURES], rowbuf[k, FEATURES : 2 * FEATURES]
            )

    def cols_in(g):
        for k in range(max(g * GROUP, 1), (g + 1) * GROUP):
            remote(colbuf.at[0, 0], colbuf.at[0, k], col_s.at[k], col_r.at[k], plane_id[k]).wait_recv()
        here = pl.ds(g * GROUP, GROUP)
        copy = remote(colbuf.at[0, here], colbuf.at[1, here], sib_s.at[g], sib_r.at[g], sibling)
        copy.start()
        return copy

    def columns_of(groups):
        blocks = [(core, j) for core, g in groups for j in range(g * GROUP, (g + 1) * GROUP)]
        b = [
            col_features(colbuf[core, j, 0:FEATURES], colbuf[core, j, FEATURES : 2 * FEATURES])
            for core, j in blocks
        ]
        d = [colbuf[core, j, 2 * FEATURES : MSG] for core, j in blocks]
        return jnp.concatenate(b, axis=1).T, jnp.concatenate(d, axis=1)

    def product(b, d, rows_of=slice(None)):
        s = jnp.dot(b, feat[:, rows_of], preferred_element_type=F32)
        return jnp.dot(d, jnp.exp2(s).astype(BF), preferred_element_type=F32)

    forwards = [cols_in(0)]
    rows_in()
    forwards.append(cols_in(1))
    acc[...] = product(*columns_of(((0, 0), (0, 1))))
    forwards.append(cols_in(2))
    forwards[0].wait_recv()
    acc[...] += product(*columns_of(((0, 2), (1, 0))))
    forwards.append(cols_in(3))
    forwards[1].wait_recv()
    forwards[2].wait_recv()
    acc[...] += product(*columns_of(((1, 1), (1, 2), (0, 3))))
    forwards[3].wait_recv()
    last = ((1, 3),)

    b, d = columns_of(last)
    homes = []
    for first in (Z // 2, 0):
        rows_of = slice(first * ROWS, (first + Z // 2) * ROWS)
        acc[:, rows_of] += product(b, d, rows_of)
        for k in range(first + Z // 2 - 1, max(first, 1) - 1, -1):
            part[k] = acc[:, k * ROWS : (k + 1) * ROWS].astype(BF)
            copy = remote(part.at[k], part.at[Z + ring_back[k]], rs_s.at[k], rs_r.at[ring_back[k]], ring_id[k])
            copy.start()
            homes.append(copy)
    for copy in rows + cols + forwards:
        copy.wait_send()
    image = acc[:, 0:ROWS] + v_noise[...] * v_dir[...]
    for k in range(1, Z):
        remote(part.at[k], part.at[Z + k], rs_s.at[k], rs_r.at[k], ring_id[k]).wait_recv()
        image += part[Z + k].astype(F32)

    sums = pack(lane, total_lanes(v_dir[...] * image), 8, sums)
    sums = pack(lane, total_lanes(v_res[...] * image), 16, sums)
    sums = pack(lane, total_lanes(image * image), 24, sums)

    ar1[0] = sums
    firsts = [
        remote(ar1.at[0], ar1.at[column_back[k]], a1_s.at[k], a1_r.at[column_back[k]], column_id[k])
        for k in range(2 * Z - 1, 0, -1)
    ]
    for copy in firsts:
        copy.start()
    for copy in homes:
        copy.wait_send()
    for k in range(1, 2 * Z):
        remote(ar1.at[0], ar1.at[k], a1_s.at[k], a1_r.at[k], column_id[k]).wait_recv()
    ar2[0] = jnp.sum(ar1[...], axis=0)
    seconds = [
        remote(ar2.at[0], ar2.at[plane_back[k]], a2_s.at[k], a2_r.at[plane_back[k]], plane_id[k])
        for k in range(PLANE - 1, 0, -1)
    ]
    for copy in seconds:
        copy.start()
    for copy in firsts:
        copy.wait_send()
    for k in range(1, PLANE):
        remote(ar2.at[0], ar2.at[k], a2_s.at[k], a2_r.at[k], plane_id[k]).wait_recv()
    total = jnp.sum(ar2[...], axis=0)

    alpha = total / pltpu.roll(total, 120, 1)
    change = alpha * (alpha * pltpu.roll(total, 104, 1) - 2.0 * pltpu.roll(total, 112, 1))
    beta = (total + change) / total
    for t in range(PROBES // 8):
        at8 = slice(8 * t, 8 * t + 8)
        a = alpha[:, t : t + 1]
        o_move[at8] = a * v_dir[at8]
        o_drop[at8] = a * image[at8]
        o_push[at8] = beta[:, t : t + 1] * v_dir[at8]

    for copy in seconds:
        copy.wait_send()


def per_device(points, lengthscale, noise, solution, residual, direction):
    sems = pltpu.SemaphoreType.DMA
    out = pltpu.VMEM((PROBES, ROWS), F32)
    hbm = pl.BlockSpec(memory_space=pltpu.HBM)
    vmem = pl.BlockSpec(memory_space=pltpu.VMEM)
    sol, res, move, drop, push = pl.pallas_call(
        body,
        out_shape=(out,) * 5,
        in_specs=[hbm] * 6,
        out_specs=(vmem,) * 5,
        scratch_shapes=[
            pltpu.VMEM((FEATURES, ROWS), F32),
            pltpu.VMEM((1, FEATURES), F32),
            pltpu.VMEM((1, ROWS), F32),
            pltpu.VMEM((PROBES, ROWS), F32),
            pltpu.VMEM((Z, 2 * FEATURES, ROWS), BF),
            pltpu.VMEM((2, PLANE, MSG, ROWS), BF),
            pltpu.VMEM((FEAT, Z * ROWS), BF),
            pltpu.VMEM((PROBES, Z * ROWS), F32),
            pltpu.VMEM((2 * Z, PROBES, ROWS), BF),
            pltpu.VMEM((2 * Z, 8, 128), F32),
            pltpu.VMEM((PLANE, 8, 128), F32),
            sems((6,)),
            sems((Z,)), sems((Z,)),
            sems((PLANE,)), sems((PLANE,)),
            sems((PLANE // GROUP,)), sems((PLANE // GROUP,)),
            sems((Z,)), sems((Z,)),
            sems((2 * Z,)), sems((2 * Z,)),
            sems((PLANE,)), sems((PLANE,)),
        ],
        compiler_params=pltpu.CompilerParams(
            collective_id=0, has_side_effects=True, vmem_limit_bytes=32 << 20
        ),
    )(
        *(
            pltpu.with_memory_space_constraint(v, pltpu.HBM)
            for v in (points.T, lengthscale[None, :], noise[None, :], solution.T, residual.T, direction.T)
        )
    )
    new_residual = res - drop
    return (sol + move).T, new_residual.T, (new_residual + push).T


def solution(mesh):
    placed = (P("blk", None), P(), P("blk"), P("blk", None), P("blk", None), P("blk", None))
    return jax.shard_map(
        per_device,
        mesh=mesh,
        in_specs=placed,
        out_specs=(P("blk", None), P("blk", None), P("blk", None)),
        check_vma=False,
    )
```

```python
import functools
import math

import jax
import jax.numpy as jnp
from jax import lax
from jax.experimental import pallas as pl
from jax.experimental.pallas import tpu as pltpu
from jax.sharding import PartitionSpec as P

ROWS = 128
FEATURES = 16
PROBES = 64
X, Y, Z = 4, 4, 8
PLANE = X * Y
MSG = 2 * FEATURES + PROBES
FEAT = 5 * FEATURES
GROUP = 4
ROOT_LOG2E = math.sqrt(math.log2(math.e))
MESH = pl.DeviceIdType.MESH
BF = jnp.bfloat16
F32 = jnp.float32


def norm_rows(hi, lo, own_first):
    s = hi.astype(F32) + lo.astype(F32)
    n = -0.5 * jnp.sum(s * s, axis=0, keepdims=True)
    n1 = n.astype(BF).astype(F32)
    n2 = (n - n1).astype(BF).astype(F32)
    n3 = n - n1 - n2
    row = lax.broadcasted_iota(jnp.int32, (FEATURES, hi.shape[1]), 0)
    at = 0 if own_first else 3
    out = jnp.where((row >= 3 - at) & (row < 6 - at), 1.0, 0.0)
    for step, part in enumerate((n1, n2, n3)):
        out = jnp.where(row == at + step, part, out)
    return out.astype(BF)


def row_features(hi, lo):
    return jnp.concatenate([hi, hi, lo, lo, norm_rows(hi, lo, True)], axis=0)


def col_features(hi, lo):
    return jnp.concatenate([hi, lo, hi, lo, norm_rows(hi, lo, False)], axis=0)


def total_lanes(v):
    return jnp.sum(v, axis=1, keepdims=True)


def pack(lane, cols, first, out):
    for t in range(PROBES // 8):
        out = jnp.where(lane == first + t, cols[8 * t : 8 * t + 8], out)
    return out


def body(
    pts, ls, noise, sol, res, dirn,
    v_sol, v_res, o_move, o_drop, o_push,
    v_pts, v_ls, v_noise, v_dir,
    rowbuf, colbuf, feat, acc, part, ar1, ar2,
    in_sem, row_s, row_r, col_s, col_r, sib_s, sib_r, rs_s, rs_r, a1_s, a1_r, a2_s, a2_r,
):
    me = lax.axis_index("blk")
    c = lax.rem(me, 2)
    z = lax.rem(me // 2, Z)
    y = lax.rem(me // (2 * Z), Y)
    x = me // (2 * Z * Y)

    def at(dx, dy, dz, dc):
        cc = c if dc == 0 else 1 - c
        zz = lax.rem(z + dz, Z)
        yy = lax.rem(y + dy, Y)
        xx = lax.rem(x + dx, X)
        return ((xx * Y + yy) * Z + zz) * 2 + cc

    def hops(dx, dy, dz):
        return min(dx, X - dx) + min(dy, Y - dy) + min(dz, Z - dz)

    plane = sorted(((k // Y, k % Y) for k in range(PLANE)), key=lambda o: hops(o[0], o[1], 0))
    ring = sorted(range(Z), key=lambda dz: hops(0, 0, dz))
    column = sorted(((dz, dc) for dz in range(Z) for dc in range(2)), key=lambda o: 2 * hops(0, 0, o[0]) + o[1])
    plane_id = [at(dx, dy, 0, 0) for dx, dy in plane]
    ring_id = [at(0, 0, dz, 0) for dz in ring]
    column_id = [at(0, 0, dz, dc) for dz, dc in column]
    sibling = at(0, 0, 0, 1)
    plane_back = [plane.index(((X - dx) % X, (Y - dy) % Y)) for dx, dy in plane]
    ring_back = [ring.index((Z - dz) % Z) for dz in ring]
    column_back = [column.index(((Z - dz) % Z, dc)) for dz, dc in column]

    def remote(src, dst, s, r, dev):
        return pltpu.make_async_remote_copy(
            src_ref=src, dst_ref=dst, send_sem=s, recv_sem=r, device_id=(dev,), device_id_type=MESH
        )

    barrier = pltpu.get_barrier_semaphore()
    for dev in ring_id[:0:-1] + plane_id[:0:-1] + [sibling]:
        pl.semaphore_signal(barrier, inc=1, device_id=(dev,), device_id_type=MESH)
    loads = [
        pltpu.make_async_copy(src, dst, in_sem.at[i])
        for i, (src, dst) in enumerate(
            ((pts, v_pts), (ls, v_ls), (dirn, v_dir), (res, v_res), (noise, v_noise), (sol, v_sol))
        )
    ]
    for load in loads:
        load.start()

    loads[0].wait()
    loads[1].wait()
    eye = lax.broadcasted_iota(jnp.int32, (FEATURES, FEATURES), 0) == lax.broadcasted_iota(
        jnp.int32, (FEATURES, FEATURES), 1
    )
    scale = total_lanes(jnp.where(eye, jnp.broadcast_to(v_ls[...], (FEATURES, FEATURES)), 0.0))
    scaled = v_pts[...] / scale * ROOT_LOG2E
    hi = scaled.astype(BF)
    lo = (scaled - hi.astype(F32)).astype(BF)
    rowbuf[0, 0:FEATURES] = hi
    rowbuf[0, FEATURES : 2 * FEATURES] = lo
    colbuf[0, 0, 0:FEATURES] = hi
    colbuf[0, 0, FEATURES : 2 * FEATURES] = lo
    loads[2].wait()
    colbuf[0, 0, 2 * FEATURES : MSG] = v_dir[...].astype(BF)

    pl.semaphore_wait(barrier, PLANE + Z - 1)
    rows = [
        remote(rowbuf.at[0], rowbuf.at[ring_back[k]], row_s.at[0], row_r.at[0], ring_id[k])
        for k in range(Z - 1, 0, -1)
    ]
    cols = [
        remote(
            colbuf.at[0, 0],
            colbuf.at[0, plane_back[k]],
            col_s.at[0],
            col_r.at[plane_back[k] // GROUP],
            plane_id[k],
        )
        for k in range(1, PLANE)
    ]
    for copy in cols[:4] + rows + cols[4:]:
        copy.start()

    others = pl.ds(1, Z - 1)
    all_rows = remote(rowbuf.at[others], rowbuf.at[others], row_s.at[0], row_r.at[0], sibling)
    others = pl.ds(1, PLANE - 1)
    all_cols = remote(colbuf.at[0, others], colbuf.at[0, others], col_s.at[0], col_r.at[0], sibling)

    for load in loads[3:]:
        load.wait()
    lane = lax.broadcasted_iota(jnp.int32, (8, 128), 1)
    sums = pack(lane, total_lanes(v_res[...] * v_res[...]), 0, jnp.zeros((8, 128), F32))

    def rows_in():
        all_rows.wait_recv()
        for k in range(Z):
            feat[:, k * ROWS : (k + 1) * ROWS] = row_features(
                rowbuf[k, 0:FEATURES], rowbuf[k, FEATURES : 2 * FEATURES]
            )

    def cols_in(g):
        first = max(g * GROUP, 1)
        came = colbuf.at[0, pl.ds(first, (g + 1) * GROUP - first)]
        remote(came, came, col_s.at[0], col_r.at[g], sibling).wait_recv()
        here = pl.ds(g * GROUP, GROUP)
        copy = remote(colbuf.at[0, here], colbuf.at[1, here], sib_s.at[g], sib_r.at[g], sibling)
        copy.start()
        return copy

    def columns_of(groups):
        blocks = [(core, j) for core, g in groups for j in range(g * GROUP, (g + 1) * GROUP)]
        b = [
            col_features(colbuf[core, j, 0:FEATURES], colbuf[core, j, FEATURES : 2 * FEATURES])
            for core, j in blocks
        ]
        d = [colbuf[core, j, 2 * FEATURES : MSG] for core, j in blocks]
        return jnp.concatenate(b, axis=1).T, jnp.concatenate(d, axis=1)

    def product(b, d, rows_of=slice(None)):
        s = jnp.dot(b, feat[:, rows_of], preferred_element_type=F32)
        return jnp.dot(d, jnp.exp2(s).astype(BF), preferred_element_type=F32)

    forwards = [cols_in(0)]
    rows_in()
    acc[...] = product(*columns_of(((0, 0),)))
    forwards.append(cols_in(1))
    forwards[0].wait_recv()
    acc[...] += product(*columns_of(((0, 1), (1, 0))))
    forwards.append(cols_in(2))
    forwards[1].wait_recv()
    acc[...] += product(*columns_of(((0, 2), (1, 1))))
    forwards.append(cols_in(3))
    forwards[2].wait_recv()
    acc[...] += product(*columns_of(((1, 2), (0, 3))))
    forwards[3].wait_recv()
    last = ((1, 3),)

    b, d = columns_of(last)
    for first in (Z // 2, 0):
        rows_of = slice(first * ROWS, (first + Z // 2) * ROWS)
        acc[:, rows_of] += product(b, d, rows_of)
        for k in range(first + Z // 2 - 1, max(first, 1) - 1, -1):
            part[k] = acc[:, k * ROWS : (k + 1) * ROWS].astype(BF)
            copy = remote(part.at[k], part.at[Z + ring_back[k]], rs_s.at[0], rs_r.at[0], ring_id[k])
            copy.start()
    for copy in [all_rows, all_cols] + forwards:
        copy.wait_send()
    image = acc[:, 0:ROWS] + v_noise[...] * v_dir[...]
    home = remote(
        part.at[pl.ds(1, Z - 1)], part.at[pl.ds(Z + 1, Z - 1)], rs_s.at[0], rs_r.at[0], sibling
    )
    home.wait_recv()
    for k in range(1, Z):
        image += part[Z + k].astype(F32)

    sums = pack(lane, total_lanes(v_dir[...] * image), 8, sums)
    sums = pack(lane, total_lanes(v_res[...] * image), 16, sums)
    sums = pack(lane, total_lanes(image * image), 24, sums)

    ar1[0] = sums
    firsts = [
        remote(ar1.at[0], ar1.at[column_back[k]], a1_s.at[0], a1_r.at[0], column_id[k])
        for k in range(2 * Z - 1, 0, -1)
    ]
    for copy in firsts:
        copy.start()
    home.wait_send()
    others = pl.ds(1, 2 * Z - 1)
    arrived = remote(ar1.at[others], ar1.at[others], a1_s.at[0], a1_r.at[0], sibling)
    arrived.wait_recv()
    ar2[0] = jnp.sum(ar1[...], axis=0)
    seconds = [
        remote(ar2.at[0], ar2.at[plane_back[k]], a2_s.at[0], a2_r.at[0], plane_id[k])
        for k in range(PLANE - 1, 0, -1)
    ]
    for copy in seconds:
        copy.start()
    arrived.wait_send()
    others = pl.ds(1, PLANE - 1)
    finished = remote(ar2.at[others], ar2.at[others], a2_s.at[0], a2_r.at[0], sibling)
    finished.wait_recv()
    total = jnp.sum(ar2[...], axis=0)

    alpha = total / pltpu.roll(total, 120, 1)
    change = alpha * (alpha * pltpu.roll(total, 104, 1) - 2.0 * pltpu.roll(total, 112, 1))
    beta = (total + change) / total
    for t in range(PROBES // 8):
        at8 = slice(8 * t, 8 * t + 8)
        a = alpha[:, t : t + 1]
        o_move[at8] = a * v_dir[at8]
        o_drop[at8] = a * image[at8]
        o_push[at8] = beta[:, t : t + 1] * v_dir[at8]

    finished.wait_send()


def per_device(points, lengthscale, noise, solution, residual, direction):
    sems = pltpu.SemaphoreType.DMA
    out = pltpu.VMEM((PROBES, ROWS), F32)
    hbm = pl.BlockSpec(memory_space=pltpu.HBM)
    vmem = pl.BlockSpec(memory_space=pltpu.VMEM)
    sol, res, move, drop, push = pl.pallas_call(
        body,
        out_shape=(out,) * 5,
        in_specs=[hbm] * 6,
        out_specs=(vmem,) * 5,
        scratch_shapes=[
            pltpu.VMEM((FEATURES, ROWS), F32),
            pltpu.VMEM((1, FEATURES), F32),
            pltpu.VMEM((1, ROWS), F32),
            pltpu.VMEM((PROBES, ROWS), F32),
            pltpu.VMEM((Z, 2 * FEATURES, ROWS), BF),
            pltpu.VMEM((2, PLANE, MSG, ROWS), BF),
            pltpu.VMEM((FEAT, Z * ROWS), BF),
            pltpu.VMEM((PROBES, Z * ROWS), F32),
            pltpu.VMEM((2 * Z, PROBES, ROWS), BF),
            pltpu.VMEM((2 * Z, 8, 128), F32),
            pltpu.VMEM((PLANE, 8, 128), F32),
            sems((6,)),
            sems((1,)), sems((1,)),
            sems((1,)), sems((PLANE // GROUP,)),
            sems((PLANE // GROUP,)), sems((PLANE // GROUP,)),
            sems((1,)), sems((1,)),
            sems((1,)), sems((1,)),
            sems((1,)), sems((1,)),
        ],
        compiler_params=pltpu.CompilerParams(
            collective_id=0, has_side_effects=True, vmem_limit_bytes=32 << 20
        ),
    )(
        *(
            pltpu.with_memory_space_constraint(v, pltpu.HBM)
            for v in (points.T, lengthscale[None, :], noise[None, :], solution.T, residual.T, direction.T)
        )
    )
    new_residual = res - drop
    return (sol + move).T, new_residual.T, (new_residual + push).T


def solution(mesh):
    placed = (P("blk", None), P(), P("blk"), P("blk", None), P("blk", None), P("blk", None))
    return jax.shard_map(
        per_device,
        mesh=mesh,
        in_specs=placed,
        out_specs=(P("blk", None), P("blk", None), P("blk", None)),
        check_vma=False,
    )
```

```python
import functools
import math

import jax
import jax.numpy as jnp
from jax import lax
from jax.experimental import pallas as pl
from jax.experimental.pallas import tpu as pltpu
from jax.sharding import PartitionSpec as P

ROWS = 128
FEATURES = 16
PROBES = 64
X, Y, Z = 4, 4, 8
PLANE = X * Y
MSG = 2 * FEATURES + PROBES
FEAT = 5 * FEATURES
GROUP = 4
ROOT_LOG2E = math.sqrt(math.log2(math.e))
MESH = pl.DeviceIdType.MESH
BF = jnp.bfloat16
F32 = jnp.float32


def norm_rows(hi, lo, own_first):
    s = hi.astype(F32) + lo.astype(F32)
    n = -0.5 * jnp.sum(s * s, axis=0, keepdims=True)
    n1 = n.astype(BF).astype(F32)
    n2 = (n - n1).astype(BF).astype(F32)
    n3 = n - n1 - n2
    row = lax.broadcasted_iota(jnp.int32, (FEATURES, hi.shape[1]), 0)
    at = 0 if own_first else 3
    out = jnp.where((row >= 3 - at) & (row < 6 - at), 1.0, 0.0)
    for step, part in enumerate((n1, n2, n3)):
        out = jnp.where(row == at + step, part, out)
    return out.astype(BF)


def row_features(hi, lo):
    return jnp.concatenate([hi, hi, lo, lo, norm_rows(hi, lo, True)], axis=0)


def col_features(hi, lo):
    return jnp.concatenate([hi, lo, hi, lo, norm_rows(hi, lo, False)], axis=0)


def total_lanes(v):
    return jnp.sum(v, axis=1, keepdims=True)


def row_sums(upper, lower):
    return jnp.sum(jnp.concatenate([upper, lower], axis=0).T, axis=0, keepdims=True)


def body(
    pts, ls, noise, sol, res, dirn,
    v_sol, v_res, o_move, o_drop, o_push,
    v_pts, v_ls, v_noise, v_dir,
    rowbuf, colbuf, feat, acc, part, ar1, ar2,
    in_sem, out_s, row_r, col_r, sib_r, rs_r, a1_r, a2_r,
):
    me = lax.axis_index("blk")
    c = lax.rem(me, 2)
    z = lax.rem(me // 2, Z)
    y = lax.rem(me // (2 * Z), Y)
    x = me // (2 * Z * Y)

    def at(dx, dy, dz, dc):
        cc = c if dc == 0 else 1 - c
        zz = lax.rem(z + dz, Z)
        yy = lax.rem(y + dy, Y)
        xx = lax.rem(x + dx, X)
        return ((xx * Y + yy) * Z + zz) * 2 + cc

    def hops(dx, dy, dz):
        return min(dx, X - dx) + min(dy, Y - dy) + min(dz, Z - dz)

    plane = sorted(((k // Y, k % Y) for k in range(PLANE)), key=lambda o: hops(o[0], o[1], 0))
    ring = sorted(range(Z), key=lambda dz: hops(0, 0, dz))
    column = sorted(((dz, dc) for dz in range(Z) for dc in range(2)), key=lambda o: 2 * hops(0, 0, o[0]) + o[1])
    plane_id = [at(dx, dy, 0, 0) for dx, dy in plane]
    ring_id = [at(0, 0, dz, 0) for dz in ring]
    column_id = [at(0, 0, dz, dc) for dz, dc in column]
    sibling = at(0, 0, 0, 1)
    plane_back = [plane.index(((X - dx) % X, (Y - dy) % Y)) for dx, dy in plane]
    ring_back = [ring.index((Z - dz) % Z) for dz in ring]
    column_back = [column.index(((Z - dz) % Z, dc)) for dz, dc in column]

    def remote(src, dst, s, r, dev):
        return pltpu.make_async_remote_copy(
            src_ref=src, dst_ref=dst, send_sem=s, recv_sem=r, device_id=(dev,), device_id_type=MESH
        )

    barrier = pltpu.get_barrier_semaphore()
    for dev in ring_id[:0:-1] + plane_id[:0:-1] + [sibling]:
        pl.semaphore_signal(barrier, inc=1, device_id=(dev,), device_id_type=MESH)
    loads = [
        pltpu.make_async_copy(src, dst, in_sem.at[i % 3])
        for i, (src, dst) in enumerate(
            ((pts, v_pts), (ls, v_ls), (dirn, v_dir), (res, v_res), (noise, v_noise), (sol, v_sol))
        )
    ]
    for load in loads[:3]:
        load.start()

    loads[0].wait()
    loads[1].wait()
    eye = lax.broadcasted_iota(jnp.int32, (FEATURES, FEATURES), 0) == lax.broadcasted_iota(
        jnp.int32, (FEATURES, FEATURES), 1
    )
    scale = total_lanes(jnp.where(eye, jnp.broadcast_to(v_ls[...], (FEATURES, FEATURES)), 0.0))
    scaled = v_pts[...] / scale * ROOT_LOG2E
    hi = scaled.astype(BF)
    lo = (scaled - hi.astype(F32)).astype(BF)
    rowbuf[0, 0:FEATURES] = hi
    rowbuf[0, FEATURES : 2 * FEATURES] = lo
    colbuf[0, 0, 0:FEATURES] = hi
    colbuf[0, 0, FEATURES : 2 * FEATURES] = lo
    loads[2].wait()
    for load in loads[3:]:
        load.start()
    colbuf[0, 0, 2 * FEATURES : MSG] = v_dir[...].astype(BF)

    pl.semaphore_wait(barrier, PLANE + Z - 1)
    rows = [
        remote(rowbuf.at[0], rowbuf.at[ring_back[k]], out_s.at[0], row_r.at[0], ring_id[k])
        for k in range(Z - 1, 0, -1)
    ]
    cols = [
        remote(
            colbuf.at[0, 0],
            colbuf.at[0, plane_back[k]],
            out_s.at[1],
            col_r.at[plane_back[k] // GROUP],
            plane_id[k],
        )
        for k in range(1, PLANE)
    ]
    for copy in cols[:4] + rows + cols[4:]:
        copy.start()

    others = pl.ds(1, Z - 1)
    all_rows = remote(rowbuf.at[others], rowbuf.at[others], out_s.at[0], row_r.at[0], sibling)
    others = pl.ds(1, PLANE - 1)
    all_cols = remote(colbuf.at[0, others], colbuf.at[0, others], out_s.at[1], col_r.at[0], sibling)

    for load in loads[3:]:
        load.wait()

    def rows_in():
        all_rows.wait_recv()
        for k in range(Z):
            feat[:, k * ROWS : (k + 1) * ROWS] = row_features(
                rowbuf[k, 0:FEATURES], rowbuf[k, FEATURES : 2 * FEATURES]
            )

    def cols_in(g):
        first = max(g * GROUP, 1)
        came = colbuf.at[0, pl.ds(first, (g + 1) * GROUP - first)]
        remote(came, came, out_s.at[1], col_r.at[g], sibling).wait_recv()
        here = pl.ds(g * GROUP, GROUP)
        copy = remote(colbuf.at[0, here], colbuf.at[1, here], out_s.at[2], sib_r.at[g], sibling)
        copy.start()
        return copy

    def columns_of(groups):
        blocks = [(core, j) for core, g in groups for j in range(g * GROUP, (g + 1) * GROUP)]
        b = [
            col_features(colbuf[core, j, 0:FEATURES], colbuf[core, j, FEATURES : 2 * FEATURES])
            for core, j in blocks
        ]
        d = [colbuf[core, j, 2 * FEATURES : MSG] for core, j in blocks]
        return jnp.concatenate(b, axis=1).T, jnp.concatenate(d, axis=1)

    def product(b, d, rows_of=slice(None)):
        s = jnp.dot(b, feat[:, rows_of], preferred_element_type=F32)
        return jnp.dot(d, jnp.exp2(s).astype(BF), preferred_element_type=F32)

    forwards = [cols_in(0)]
    rows_in()
    acc[...] = product(*columns_of(((0, 0),)))
    forwards.append(cols_in(1))
    forwards[0].wait_recv()
    acc[...] += product(*columns_of(((0, 1), (1, 0))))
    forwards.append(cols_in(2))
    forwards.append(cols_in(3))
    forwards[1].wait_recv()
    acc[...] += product(*columns_of(((0, 2), (0, 3), (1, 1))))
    forwards[2].wait_recv()
    forwards[3].wait_recv()
    last = ((1, 2), (1, 3))

    b, d = columns_of(last)
    for first in (Z // 2, 0):
        rows_of = slice(first * ROWS, (first + Z // 2) * ROWS)
        acc[:, rows_of] += product(b, d, rows_of)
        for k in range(first + Z // 2 - 1, max(first, 1) - 1, -1):
            part[k] = acc[:, k * ROWS : (k + 1) * ROWS].astype(BF)
            copy = remote(part.at[k], part.at[Z + ring_back[k]], out_s.at[3], rs_r.at[0], ring_id[k])
            copy.start()
    every = remote(colbuf.at[0], colbuf.at[1], out_s.at[2], sib_r.at[0], sibling)
    for copy in (all_rows, all_cols, every):
        copy.wait_send()
    image = acc[:, 0:ROWS] + v_noise[...] * v_dir[...]
    home = remote(
        part.at[pl.ds(1, Z - 1)], part.at[pl.ds(Z + 1, Z - 1)], out_s.at[3], rs_r.at[0], sibling
    )
    home.wait_recv()
    for k in range(1, Z):
        image += part[Z + k].astype(F32)

    ar1[0, 0:1] = row_sums(v_res[...] * v_res[...], v_dir[...] * image)
    ar1[0, 1:2] = row_sums(v_res[...] * image, image * image)
    firsts = [
        remote(ar1.at[0], ar1.at[column_back[k]], out_s.at[0], a1_r.at[0], column_id[k])
        for k in range(2 * Z - 1, 0, -1)
    ]
    for copy in firsts:
        copy.start()
    home.wait_send()
    others = pl.ds(1, 2 * Z - 1)
    arrived = remote(ar1.at[others], ar1.at[others], out_s.at[0], a1_r.at[0], sibling)
    arrived.wait_recv()
    ar2[0] = jnp.sum(ar1[...], axis=0)
    seconds = [
        remote(ar2.at[0], ar2.at[plane_back[k]], out_s.at[1], a2_r.at[0], plane_id[k])
        for k in range(PLANE - 1, 0, -1)
    ]
    for copy in seconds:
        copy.start()
    arrived.wait_send()
    others = pl.ds(1, PLANE - 1)
    finished = remote(ar2.at[others], ar2.at[others], out_s.at[1], a2_r.at[0], sibling)
    finished.wait_recv()
    total = jnp.sum(ar2[...], axis=0)

    one, two = total[0:1], total[1:2]
    alpha = one / pltpu.roll(one, PROBES, 1)
    change = alpha * (alpha * pltpu.roll(two, PROBES, 1) - 2.0 * two)
    beta = (one + change) / one
    lane = lax.broadcasted_iota(jnp.int32, (1, 2 * PROBES), 1)
    both = jnp.where(lane < PROBES, alpha, pltpu.roll(beta, PROBES, 1))
    both = jnp.broadcast_to(both, (2 * PROBES, ROWS)).T
    o_move[...] = both[0:PROBES] * v_dir[...]
    o_drop[...] = both[0:PROBES] * image
    o_push[...] = both[PROBES:] * v_dir[...]

    finished.wait_send()


def per_device(points, lengthscale, noise, solution, residual, direction):
    sems = pltpu.SemaphoreType.DMA
    out = pltpu.VMEM((PROBES, ROWS), F32)
    hbm = pl.BlockSpec(memory_space=pltpu.HBM)
    vmem = pl.BlockSpec(memory_space=pltpu.VMEM)
    sol, res, move, drop, push = pl.pallas_call(
        body,
        out_shape=(out,) * 5,
        in_specs=[hbm] * 6,
        out_specs=(vmem,) * 5,
        scratch_shapes=[
            pltpu.VMEM((FEATURES, ROWS), F32),
            pltpu.VMEM((1, FEATURES), F32),
            pltpu.VMEM((1, ROWS), F32),
            pltpu.VMEM((PROBES, ROWS), F32),
            pltpu.VMEM((Z, 2 * FEATURES, ROWS), BF),
            pltpu.VMEM((2, PLANE, MSG, ROWS), BF),
            pltpu.VMEM((FEAT, Z * ROWS), BF),
            pltpu.VMEM((PROBES, Z * ROWS), F32),
            pltpu.VMEM((2 * Z, PROBES, ROWS), BF),
            pltpu.VMEM((2 * Z, 2, 2 * PROBES), F32),
            pltpu.VMEM((PLANE, 2, 2 * PROBES), F32),
            sems((3,)),
            sems((4,)),
            sems((1,)),
            sems((PLANE // GROUP,)),
            sems((PLANE // GROUP,)),
            sems((1,)),
            sems((1,)),
            sems((1,)),
        ],
        compiler_params=pltpu.CompilerParams(
            collective_id=0, has_side_effects=True, vmem_limit_bytes=32 << 20
        ),
    )(
        *(
            pltpu.with_memory_space_constraint(v, pltpu.HBM)
            for v in (points.T, lengthscale[None, :], noise[None, :], solution.T, residual.T, direction.T)
        )
    )
    new_residual = res - drop
    return (sol + move).T, new_residual.T, (new_residual + push).T


def solution(mesh):
    placed = (P("blk", None), P(), P("blk"), P("blk", None), P("blk", None), P("blk", None))
    return jax.shard_map(
        per_device,
        mesh=mesh,
        in_specs=placed,
        out_specs=(P("blk", None), P("blk", None), P("blk", None)),
        check_vma=False,
    )
```

```python
import functools
import math

import jax
import jax.numpy as jnp
from jax import lax
from jax.experimental import pallas as pl
from jax.experimental.pallas import tpu as pltpu
from jax.sharding import PartitionSpec as P

ROWS = 128
FEATURES = 16
PROBES = 64
X, Y, Z = 4, 4, 8
PLANE = X * Y
MSG = 2 * FEATURES + PROBES
FEAT = 5 * FEATURES
GROUP = 4
ROOT_LOG2E = math.sqrt(math.log2(math.e))
MESH = pl.DeviceIdType.MESH
BF = jnp.bfloat16
F32 = jnp.float32


def norm_rows(hi, lo, own_first):
    s = hi.astype(F32) + lo.astype(F32)
    n = -0.5 * jnp.sum(s * s, axis=0, keepdims=True)
    n1 = n.astype(BF).astype(F32)
    n2 = (n - n1).astype(BF).astype(F32)
    n3 = n - n1 - n2
    row = lax.broadcasted_iota(jnp.int32, (FEATURES, hi.shape[1]), 0)
    at = 0 if own_first else 3
    out = jnp.where((row >= 3 - at) & (row < 6 - at), 1.0, 0.0)
    for step, part in enumerate((n1, n2, n3)):
        out = jnp.where(row == at + step, part, out)
    return out.astype(BF)


def row_features(hi, lo):
    return jnp.concatenate([hi, hi, lo, lo, norm_rows(hi, lo, True)], axis=0)


def col_features(hi, lo):
    return jnp.concatenate([hi, lo, hi, lo, norm_rows(hi, lo, False)], axis=0)


def total_lanes(v):
    return jnp.sum(v, axis=1, keepdims=True)


def row_sums(upper, lower):
    return jnp.sum(jnp.concatenate([upper, lower], axis=0).T, axis=0, keepdims=True)


def body(
    pts, ls, noise, sol, res, dirn,
    v_sol, v_res, o_move, o_drop, o_push,
    v_pts, v_ls, v_noise, v_dir,
    rowbuf, colbuf, feat, acc, part, ar1, ar2,
    in_sem, out_s, row_r, col_r, sib_r, rs_r, a1_r, a2_r,
):
    me = lax.axis_index("blk")
    c = lax.rem(me, 2)
    z = lax.rem(me // 2, Z)
    y = lax.rem(me // (2 * Z), Y)
    x = me // (2 * Z * Y)

    def at(dx, dy, dz, dc):
        cc = c if dc == 0 else 1 - c
        zz = lax.rem(z + dz, Z)
        yy = lax.rem(y + dy, Y)
        xx = lax.rem(x + dx, X)
        return ((xx * Y + yy) * Z + zz) * 2 + cc

    def hops(dx, dy, dz):
        return min(dx, X - dx) + min(dy, Y - dy) + min(dz, Z - dz)

    plane = sorted(((k // Y, k % Y) for k in range(PLANE)), key=lambda o: hops(o[0], o[1], 0))
    ring = sorted(range(Z), key=lambda dz: hops(0, 0, dz))
    column = sorted(((dz, dc) for dz in range(Z) for dc in range(2)), key=lambda o: 2 * hops(0, 0, o[0]) + o[1])
    plane_id = [at(dx, dy, 0, 0) for dx, dy in plane]
    ring_id = [at(0, 0, dz, 0) for dz in ring]
    column_id = [at(0, 0, dz, dc) for dz, dc in column]
    sibling = at(0, 0, 0, 1)
    plane_back = [plane.index(((X - dx) % X, (Y - dy) % Y)) for dx, dy in plane]
    ring_back = [ring.index((Z - dz) % Z) for dz in ring]
    column_back = [column.index(((Z - dz) % Z, dc)) for dz, dc in column]

    def remote(src, dst, s, r, dev):
        return pltpu.make_async_remote_copy(
            src_ref=src, dst_ref=dst, send_sem=s, recv_sem=r, device_id=(dev,), device_id_type=MESH
        )

    barrier = pltpu.get_barrier_semaphore()
    for dev in ring_id[:0:-1] + plane_id[:0:-1] + [sibling]:
        pl.semaphore_signal(barrier, inc=1, device_id=(dev,), device_id_type=MESH)
    loads = [
        pltpu.make_async_copy(src, dst, in_sem.at[i % 3])
        for i, (src, dst) in enumerate(
            ((pts, v_pts), (ls, v_ls), (dirn, v_dir), (res, v_res), (noise, v_noise), (sol, v_sol))
        )
    ]
    for load in loads[:3]:
        load.start()

    loads[0].wait()
    loads[1].wait()
    eye = lax.broadcasted_iota(jnp.int32, (FEATURES, FEATURES), 0) == lax.broadcasted_iota(
        jnp.int32, (FEATURES, FEATURES), 1
    )
    scale = total_lanes(jnp.where(eye, jnp.broadcast_to(v_ls[...], (FEATURES, FEATURES)), 0.0))
    scaled = v_pts[...] / scale * ROOT_LOG2E
    hi = scaled.astype(BF)
    lo = (scaled - hi.astype(F32)).astype(BF)
    rowbuf[0, 0:FEATURES] = hi
    rowbuf[0, FEATURES : 2 * FEATURES] = lo
    colbuf[0, 0, 0:FEATURES] = hi
    colbuf[0, 0, FEATURES : 2 * FEATURES] = lo
    loads[2].wait()
    for load in loads[3:]:
        load.start()
    colbuf[0, 0, 2 * FEATURES : MSG] = v_dir[...].astype(BF)

    pl.semaphore_wait(barrier, PLANE + Z - 1)
    rows = [
        remote(rowbuf.at[0], rowbuf.at[ring_back[k]], out_s.at[0], row_r.at[0], ring_id[k])
        for k in range(Z - 1, 0, -1)
    ]
    cols = [
        remote(
            colbuf.at[0, 0],
            colbuf.at[0, plane_back[k]],
            out_s.at[1],
            col_r.at[plane_back[k] // GROUP],
            plane_id[k],
        )
        for k in range(1, PLANE)
    ]
    for copy in cols[:4] + rows + cols[4:]:
        copy.start()

    others = pl.ds(1, Z - 1)
    all_rows = remote(rowbuf.at[others], rowbuf.at[others], out_s.at[0], row_r.at[0], sibling)
    others = pl.ds(1, PLANE - 1)
    all_cols = remote(colbuf.at[0, others], colbuf.at[0, others], out_s.at[1], col_r.at[0], sibling)

    for load in loads[3:]:
        load.wait()

    def rows_in():
        all_rows.wait_recv()
        for k in range(Z):
            feat[:, k * ROWS : (k + 1) * ROWS] = row_features(
                rowbuf[k, 0:FEATURES], rowbuf[k, FEATURES : 2 * FEATURES]
            )

    def cols_in(g):
        first = max(g * GROUP, 1)
        came = colbuf.at[0, pl.ds(first, (g + 1) * GROUP - first)]
        remote(came, came, out_s.at[1], col_r.at[g], sibling).wait_recv()
        here = pl.ds(g * GROUP, GROUP)
        copy = remote(colbuf.at[0, here], colbuf.at[1, here], out_s.at[2], sib_r.at[g], sibling)
        copy.start()
        return copy

    def columns_of(groups):
        blocks = [(core, j) for core, g in groups for j in range(g * GROUP, (g + 1) * GROUP)]
        b = [
            col_features(colbuf[core, j, 0:FEATURES], colbuf[core, j, FEATURES : 2 * FEATURES])
            for core, j in blocks
        ]
        d = [colbuf[core, j, 2 * FEATURES : MSG] for core, j in blocks]
        return jnp.concatenate(b, axis=1).T, jnp.concatenate(d, axis=1)

    def product(b, d, rows_of=slice(None)):
        s = jnp.dot(b, feat[:, rows_of], preferred_element_type=F32)
        return jnp.dot(d, jnp.exp2(s).astype(BF), preferred_element_type=F32)

    forwards = [cols_in(0)]
    rows_in()
    acc[...] = product(*columns_of(((0, 0),)))
    forwards.append(cols_in(1))
    forwards[0].wait_recv()
    acc[...] += product(*columns_of(((0, 1), (1, 0))))
    forwards.append(cols_in(2))
    forwards.append(cols_in(3))
    forwards[1].wait_recv()
    late = columns_of(((0, 2), (0, 3), (1, 1)))
    far, near = slice(Z // 2 * ROWS, Z * ROWS), slice(0, Z // 2 * ROWS)
    acc[:, far] += product(*late, far)
    forwards[2].wait_recv()
    forwards[3].wait_recv()

    last = columns_of(((1, 2), (1, 3)))

    def send_home(first, end):
        for k in range(end - 1, first - 1, -1):
            part[k] = acc[:, k * ROWS : (k + 1) * ROWS].astype(BF)
            remote(
                part.at[k], part.at[Z + ring_back[k]], out_s.at[3], rs_r.at[0], ring_id[k]
            ).start()

    acc[:, far] += product(*last, far)
    send_home(Z // 2, Z)
    acc[:, near] += product(*late, near) + product(*last, near)
    send_home(1, Z // 2)
    every = remote(colbuf.at[0], colbuf.at[1], out_s.at[2], sib_r.at[0], sibling)
    for copy in (all_rows, all_cols, every):
        copy.wait_send()
    image = acc[:, 0:ROWS] + v_noise[...] * v_dir[...]
    home = remote(
        part.at[pl.ds(1, Z - 1)], part.at[pl.ds(Z + 1, Z - 1)], out_s.at[3], rs_r.at[0], sibling
    )
    home.wait_recv()
    for k in range(1, Z):
        image += part[Z + k].astype(F32)

    ar1[0, 0:1] = row_sums(v_res[...] * v_res[...], v_dir[...] * image)
    ar1[0, 1:2] = row_sums(v_res[...] * image, image * image)
    firsts = [
        remote(ar1.at[0], ar1.at[column_back[k]], out_s.at[0], a1_r.at[0], column_id[k])
        for k in range(2 * Z - 1, 0, -1)
    ]
    for copy in firsts:
        copy.start()
    home.wait_send()
    others = pl.ds(1, 2 * Z - 1)
    arrived = remote(ar1.at[others], ar1.at[others], out_s.at[0], a1_r.at[0], sibling)
    arrived.wait_recv()
    ar2[0] = jnp.sum(ar1[...], axis=0)
    seconds = [
        remote(ar2.at[0], ar2.at[plane_back[k]], out_s.at[1], a2_r.at[0], plane_id[k])
        for k in range(PLANE - 1, 0, -1)
    ]
    for copy in seconds:
        copy.start()
    arrived.wait_send()
    others = pl.ds(1, PLANE - 1)
    finished = remote(ar2.at[others], ar2.at[others], out_s.at[1], a2_r.at[0], sibling)
    finished.wait_recv()
    total = jnp.sum(ar2[...], axis=0)

    one, two = total[0:1], total[1:2]
    alpha = one / pltpu.roll(one, PROBES, 1)
    change = alpha * (alpha * pltpu.roll(two, PROBES, 1) - 2.0 * two)
    beta = (one + change) / one
    lane = lax.broadcasted_iota(jnp.int32, (1, 2 * PROBES), 1)
    both = jnp.where(lane < PROBES, alpha, pltpu.roll(beta, PROBES, 1))
    both = jnp.broadcast_to(both, (2 * PROBES, ROWS)).T
    o_move[...] = both[0:PROBES] * v_dir[...]
    o_drop[...] = both[0:PROBES] * image
    o_push[...] = both[PROBES:] * v_dir[...]

    finished.wait_send()


def per_device(points, lengthscale, noise, solution, residual, direction):
    sems = pltpu.SemaphoreType.DMA
    out = pltpu.VMEM((PROBES, ROWS), F32)
    hbm = pl.BlockSpec(memory_space=pltpu.HBM)
    vmem = pl.BlockSpec(memory_space=pltpu.VMEM)
    sol, res, move, drop, push = pl.pallas_call(
        body,
        out_shape=(out,) * 5,
        in_specs=[hbm] * 6,
        out_specs=(vmem,) * 5,
        scratch_shapes=[
            pltpu.VMEM((FEATURES, ROWS), F32),
            pltpu.VMEM((1, FEATURES), F32),
            pltpu.VMEM((1, ROWS), F32),
            pltpu.VMEM((PROBES, ROWS), F32),
            pltpu.VMEM((Z, 2 * FEATURES, ROWS), BF),
            pltpu.VMEM((2, PLANE, MSG, ROWS), BF),
            pltpu.VMEM((FEAT, Z * ROWS), BF),
            pltpu.VMEM((PROBES, Z * ROWS), F32),
            pltpu.VMEM((2 * Z, PROBES, ROWS), BF),
            pltpu.VMEM((2 * Z, 2, 2 * PROBES), F32),
            pltpu.VMEM((PLANE, 2, 2 * PROBES), F32),
            sems((3,)),
            sems((4,)),
            sems((1,)),
            sems((PLANE // GROUP,)),
            sems((PLANE // GROUP,)),
            sems((1,)),
            sems((1,)),
            sems((1,)),
        ],
        compiler_params=pltpu.CompilerParams(
            collective_id=0, has_side_effects=True, vmem_limit_bytes=32 << 20
        ),
    )(
        *(
            pltpu.with_memory_space_constraint(v, pltpu.HBM)
            for v in (points.T, lengthscale[None, :], noise[None, :], solution.T, residual.T, direction.T)
        )
    )
    new_residual = res - drop
    return (sol + move).T, new_residual.T, (new_residual + push).T


def solution(mesh):
    placed = (P("blk", None), P(), P("blk"), P("blk", None), P("blk", None), P("blk", None))
    return jax.shard_map(
        per_device,
        mesh=mesh,
        in_specs=placed,
        out_specs=(P("blk", None), P("blk", None), P("blk", None)),
        check_vma=False,
    )
```

```python
import functools
import math

import jax
import jax.numpy as jnp
from jax import lax
from jax.experimental import pallas as pl
from jax.experimental.pallas import tpu as pltpu
from jax.sharding import PartitionSpec as P

ROWS = 128
FEATURES = 16
PROBES = 64
X, Y, Z = 4, 4, 8
PLANE = X * Y
MSG = 2 * FEATURES + PROBES
FEAT = 5 * FEATURES
CUTS = (0, 5, 11, 16)
ROOT_LOG2E = math.sqrt(math.log2(math.e))
MESH = pl.DeviceIdType.MESH
BF = jnp.bfloat16
F32 = jnp.float32


def norm_rows(hi, lo, own_first):
    s = hi.astype(F32) + lo.astype(F32)
    n = -0.5 * jnp.sum(s * s, axis=0, keepdims=True)
    n1 = n.astype(BF).astype(F32)
    n2 = (n - n1).astype(BF).astype(F32)
    n3 = n - n1 - n2
    row = lax.broadcasted_iota(jnp.int32, (FEATURES, hi.shape[1]), 0)
    at = 0 if own_first else 3
    out = jnp.where((row >= 3 - at) & (row < 6 - at), 1.0, 0.0)
    for step, part in enumerate((n1, n2, n3)):
        out = jnp.where(row == at + step, part, out)
    return out.astype(BF)


def row_features(hi, lo):
    return jnp.concatenate([hi, hi, lo, lo, norm_rows(hi, lo, True)], axis=0)


def col_features(hi, lo):
    return jnp.concatenate([hi, lo, hi, lo, norm_rows(hi, lo, False)], axis=0)


def total_lanes(v):
    return jnp.sum(v, axis=1, keepdims=True)


def row_sums(upper, lower):
    return jnp.sum(jnp.concatenate([upper, lower], axis=0).T, axis=0, keepdims=True)


def body(
    pts, ls, noise, sol, res, dirn,
    v_sol, v_res, o_move, o_drop, o_push,
    v_pts, v_ls, v_noise, v_dir,
    rowbuf, colbuf, feat, acc, part, ar1, ar2,
    in_sem, out_s, row_r, col_r, sib_r, rs_r, a1_r, a2_r,
):
    me = lax.axis_index("blk")
    c = lax.rem(me, 2)
    z = lax.rem(me // 2, Z)
    y = lax.rem(me // (2 * Z), Y)
    x = me // (2 * Z * Y)

    def at(dx, dy, dz, dc):
        cc = c if dc == 0 else 1 - c
        zz = lax.rem(z + dz, Z)
        yy = lax.rem(y + dy, Y)
        xx = lax.rem(x + dx, X)
        return ((xx * Y + yy) * Z + zz) * 2 + cc

    def hops(dx, dy, dz):
        return min(dx, X - dx) + min(dy, Y - dy) + min(dz, Z - dz)

    plane = sorted(((k // Y, k % Y) for k in range(PLANE)), key=lambda o: hops(o[0], o[1], 0))
    ring = sorted(range(Z), key=lambda dz: hops(0, 0, dz))
    column = sorted(((dz, dc) for dz in range(Z) for dc in range(2)), key=lambda o: 2 * hops(0, 0, o[0]) + o[1])
    plane_id = [at(dx, dy, 0, 0) for dx, dy in plane]
    ring_id = [at(0, 0, dz, 0) for dz in ring]
    column_id = [at(0, 0, dz, dc) for dz, dc in column]
    sibling = at(0, 0, 0, 1)
    plane_back = [plane.index(((X - dx) % X, (Y - dy) % Y)) for dx, dy in plane]
    ring_back = [ring.index((Z - dz) % Z) for dz in ring]
    column_back = [column.index(((Z - dz) % Z, dc)) for dz, dc in column]

    def remote(src, dst, s, r, dev):
        return pltpu.make_async_remote_copy(
            src_ref=src, dst_ref=dst, send_sem=s, recv_sem=r, device_id=(dev,), device_id_type=MESH
        )

    barrier = pltpu.get_barrier_semaphore()
    for dev in ring_id[:0:-1] + plane_id[:0:-1] + [sibling]:
        pl.semaphore_signal(barrier, inc=1, device_id=(dev,), device_id_type=MESH)
    loads = [
        pltpu.make_async_copy(src, dst, in_sem.at[i % 3])
        for i, (src, dst) in enumerate(
            ((pts, v_pts), (ls, v_ls), (dirn, v_dir), (res, v_res), (noise, v_noise), (sol, v_sol))
        )
    ]
    for load in loads[:3]:
        load.start()

    loads[0].wait()
    loads[1].wait()
    eye = lax.broadcasted_iota(jnp.int32, (FEATURES, FEATURES), 0) == lax.broadcasted_iota(
        jnp.int32, (FEATURES, FEATURES), 1
    )
    scale = total_lanes(jnp.where(eye, jnp.broadcast_to(v_ls[...], (FEATURES, FEATURES)), 0.0))
    scaled = v_pts[...] / scale * ROOT_LOG2E
    hi = scaled.astype(BF)
    lo = (scaled - hi.astype(F32)).astype(BF)
    rowbuf[0, 0:FEATURES] = hi
    rowbuf[0, FEATURES : 2 * FEATURES] = lo
    colbuf[0, 0, 0:FEATURES] = hi
    colbuf[0, 0, FEATURES : 2 * FEATURES] = lo
    loads[2].wait()
    for load in loads[3:]:
        load.start()
    colbuf[0, 0, 2 * FEATURES : MSG] = v_dir[...].astype(BF)

    pl.semaphore_wait(barrier, PLANE + Z - 1)
    rows = [
        remote(rowbuf.at[0], rowbuf.at[ring_back[k]], out_s.at[0], row_r.at[0], ring_id[k])
        for k in range(Z - 1, 0, -1)
    ]
    cols = [
        remote(
            colbuf.at[0, 0],
            colbuf.at[0, plane_back[k]],
            out_s.at[1],
            col_r.at[sum(plane_back[k] >= cut for cut in CUTS[1:])],
            plane_id[k],
        )
        for k in range(1, PLANE)
    ]
    for copy in cols[:4] + rows + cols[4:]:
        copy.start()

    others = pl.ds(1, Z - 1)
    all_rows = remote(rowbuf.at[others], rowbuf.at[others], out_s.at[0], row_r.at[0], sibling)
    others = pl.ds(1, PLANE - 1)
    all_cols = remote(colbuf.at[0, others], colbuf.at[0, others], out_s.at[1], col_r.at[0], sibling)

    for load in loads[3:]:
        load.wait()

    def rows_in():
        all_rows.wait_recv()
        for k in range(Z):
            feat[:, k * ROWS : (k + 1) * ROWS] = row_features(
                rowbuf[k, 0:FEATURES], rowbuf[k, FEATURES : 2 * FEATURES]
            )

    def cols_in(g):
        first = max(CUTS[g], 1)
        came = colbuf.at[0, pl.ds(first, CUTS[g + 1] - first)]
        remote(came, came, out_s.at[1], col_r.at[g], sibling).wait_recv()
        here = pl.ds(CUTS[g], CUTS[g + 1] - CUTS[g])
        copy = remote(colbuf.at[0, here], colbuf.at[1, here], out_s.at[2], sib_r.at[g], sibling)
        copy.start()
        return copy

    def columns_of(groups):
        blocks = [(core, j) for core, g in groups for j in range(CUTS[g], CUTS[g + 1])]
        b = [
            col_features(colbuf[core, j, 0:FEATURES], colbuf[core, j, FEATURES : 2 * FEATURES])
            for core, j in blocks
        ]
        d = [colbuf[core, j, 2 * FEATURES : MSG] for core, j in blocks]
        return jnp.concatenate(b, axis=1).T, jnp.concatenate(d, axis=1)

    def product(b, d, rows_of=slice(None)):
        s = jnp.dot(b, feat[:, rows_of], preferred_element_type=F32)
        return jnp.dot(d, jnp.exp2(s).astype(BF), preferred_element_type=F32)

    forwards = [cols_in(0)]
    rows_in()
    acc[...] = product(*columns_of(((0, 0),)))
    forwards.append(cols_in(1))
    forwards[0].wait_recv()
    acc[...] += product(*columns_of(((1, 0),)))
    forwards.append(cols_in(2))
    late = columns_of(((0, 1), (0, 2)))
    far, near = slice(Z // 2 * ROWS, Z * ROWS), slice(0, Z // 2 * ROWS)
    acc[:, far] += product(*late, far)
    forwards[1].wait_recv()
    forwards[2].wait_recv()

    last = columns_of(((1, 1), (1, 2)))

    def send_home(first, end):
        for k in range(end - 1, first - 1, -1):
            part[k] = acc[:, k * ROWS : (k + 1) * ROWS].astype(BF)
            remote(
                part.at[k], part.at[Z + ring_back[k]], out_s.at[3], rs_r.at[0], ring_id[k]
            ).start()

    acc[:, far] += product(*last, far)
    send_home(Z // 2, Z)
    acc[:, near] += product(*late, near) + product(*last, near)
    send_home(1, Z // 2)
    every = remote(colbuf.at[0], colbuf.at[1], out_s.at[2], sib_r.at[0], sibling)
    for copy in (all_rows, all_cols, every):
        copy.wait_send()
    image = acc[:, 0:ROWS] + v_noise[...] * v_dir[...]
    home = remote(
        part.at[pl.ds(1, Z - 1)], part.at[pl.ds(Z + 1, Z - 1)], out_s.at[3], rs_r.at[0], sibling
    )
    home.wait_recv()
    for k in range(1, Z):
        image += part[Z + k].astype(F32)

    ar1[0, 0:1] = row_sums(v_res[...] * v_res[...], v_dir[...] * image)
    ar1[0, 1:2] = row_sums(v_res[...] * image, image * image)
    firsts = [
        remote(ar1.at[0], ar1.at[column_back[k]], out_s.at[0], a1_r.at[0], column_id[k])
        for k in range(2 * Z - 1, 0, -1)
    ]
    for copy in firsts:
        copy.start()
    home.wait_send()
    others = pl.ds(1, 2 * Z - 1)
    arrived = remote(ar1.at[others], ar1.at[others], out_s.at[0], a1_r.at[0], sibling)
    arrived.wait_recv()
    ar2[0] = jnp.sum(ar1[...], axis=0)
    seconds = [
        remote(ar2.at[0], ar2.at[plane_back[k]], out_s.at[1], a2_r.at[0], plane_id[k])
        for k in range(PLANE - 1, 0, -1)
    ]
    for copy in seconds:
        copy.start()
    arrived.wait_send()
    others = pl.ds(1, PLANE - 1)
    finished = remote(ar2.at[others], ar2.at[others], out_s.at[1], a2_r.at[0], sibling)
    finished.wait_recv()
    total = jnp.sum(ar2[...], axis=0)

    one, two = total[0:1], total[1:2]
    alpha = one / pltpu.roll(one, PROBES, 1)
    change = alpha * (alpha * pltpu.roll(two, PROBES, 1) - 2.0 * two)
    beta = (one + change) / one
    lane = lax.broadcasted_iota(jnp.int32, (1, 2 * PROBES), 1)
    both = jnp.where(lane < PROBES, alpha, pltpu.roll(beta, PROBES, 1))
    both = jnp.broadcast_to(both, (2 * PROBES, ROWS)).T
    o_move[...] = both[0:PROBES] * v_dir[...]
    o_drop[...] = both[0:PROBES] * image
    o_push[...] = both[PROBES:] * v_dir[...]

    finished.wait_send()


def per_device(points, lengthscale, noise, solution, residual, direction):
    sems = pltpu.SemaphoreType.DMA
    out = pltpu.VMEM((PROBES, ROWS), F32)
    hbm = pl.BlockSpec(memory_space=pltpu.HBM)
    vmem = pl.BlockSpec(memory_space=pltpu.VMEM)
    sol, res, move, drop, push = pl.pallas_call(
        body,
        out_shape=(out,) * 5,
        in_specs=[hbm] * 6,
        out_specs=(vmem,) * 5,
        scratch_shapes=[
            pltpu.VMEM((FEATURES, ROWS), F32),
            pltpu.VMEM((1, FEATURES), F32),
            pltpu.VMEM((1, ROWS), F32),
            pltpu.VMEM((PROBES, ROWS), F32),
            pltpu.VMEM((Z, 2 * FEATURES, ROWS), BF),
            pltpu.VMEM((2, PLANE, MSG, ROWS), BF),
            pltpu.VMEM((FEAT, Z * ROWS), BF),
            pltpu.VMEM((PROBES, Z * ROWS), F32),
            pltpu.VMEM((2 * Z, PROBES, ROWS), BF),
            pltpu.VMEM((2 * Z, 2, 2 * PROBES), F32),
            pltpu.VMEM((PLANE, 2, 2 * PROBES), F32),
            sems((3,)),
            sems((4,)),
            sems((1,)),
            sems((len(CUTS) - 1,)),
            sems((len(CUTS) - 1,)),
            sems((1,)),
            sems((1,)),
            sems((1,)),
        ],
        compiler_params=pltpu.CompilerParams(
            collective_id=0, has_side_effects=True, vmem_limit_bytes=32 << 20
        ),
    )(
        *(
            pltpu.with_memory_space_constraint(v, pltpu.HBM)
            for v in (points.T, lengthscale[None, :], noise[None, :], solution.T, residual.T, direction.T)
        )
    )
    new_residual = res - drop
    return (sol + move).T, new_residual.T, (new_residual + push).T


def solution(mesh):
    placed = (P("blk", None), P(), P("blk"), P("blk", None), P("blk", None), P("blk", None))
    return jax.shard_map(
        per_device,
        mesh=mesh,
        in_specs=placed,
        out_specs=(P("blk", None), P("blk", None), P("blk", None)),
        check_vma=False,
    )
```
